32 devices in a mesh: seq: 16 (over z, x, core), store: 2 (over y).
Axes of the slice: x: 2, y: 2, z: 4, core: 2. Of those that a mesh axis runs over, the one named last changes fastest.
Arguments:
- queries: bfloat16 [2, 2048, 4096], P('store', 'seq'), may hold values from -12 to 12
- keys: bfloat16 [2, 2048, 512], P('store', 'seq'), may hold values from -6 to 6
- values: bfloat16 [2, 2048, 512], P('store', 'seq'), may hold values from -6 to 6
- segment_ids: int32 [2, 2048], P('store', 'seq'), may hold values from 0 to 3, never falling along the last dimension, each value on 1 to 1024 neighbouring positions
- route_ids: int32 [2, 2048], P('store', 'seq'), may hold values from 0 to 511, as said below
- adapter_down: bfloat16 [4096, 32768], P(None, ('seq', 'store')), may hold values from -0.09375 to 0.09375
- adapter_up: bfloat16 [32768, 4096], P(('seq', 'store')), may hold values from -0.75 to 0.75
Outputs:
- mixed: bfloat16 [2, 2048, 4096], P('store', 'seq')
The draws below stay inside these ranges and needn't reach their ends.
Inputs may be any that keep to these rules, and one draw needn't show every extreme that they name: `route_ids`: among the 128 tokens of one device (positions j * 128 to j * 128 + 127 of one sequence), at most 8 name adapters of any one owner, the owner of adapter e being the device of flat index e // 16 over seq then store; in every draw some owner gets exactly 8 tokens from every device.
All inputs are finite; a program needn't handle non-finite values.
Results may differ from the reference program's by a relative error of at most 0.006.
Values may be sent and summed in bfloat16 or wider, within the bound.
A program may use at most 128 MiB of HBM per device.

```python
import math
import jax
import jax.numpy as jnp
import numpy as np
from jax import lax

HEAD_DIM = 128
HEADS = 32
KV_HEADS = 4
RANK = 64
EXP_DEV = 16
TOK_DEV = 128
WIDTH = 4096
LENGTH = 2048
EXPERTS = 512
CAP = 8
N_SEQ = 16
N_STORE = 2
DEVICES = 32


def draw_queries(key, part):
    inner = jax.random.fold_in(key, 11)
    field = 2.5 * jnp.clip(jax.random.normal(inner, (N_STORE, LENGTH, HEADS, HEAD_DIM), jnp.float32), -4.8, 4.8)
    return field.reshape(N_STORE, LENGTH, HEADS * HEAD_DIM).astype(jnp.bfloat16)


def draw_keys(key, part):
    inner = jax.random.fold_in(key, 13)
    field = jnp.clip(jax.random.normal(inner, (N_STORE, LENGTH, KV_HEADS, HEAD_DIM), jnp.float32), -6.0, 6.0)
    return field.reshape(N_STORE, LENGTH, KV_HEADS * HEAD_DIM).astype(jnp.bfloat16)


def draw_route_ids(key, part):
    hot_owner = jax.random.randint(jax.random.fold_in(key, 21), (), 0, DEVICES)

    def one_block(block_key):
        first, second, third = jax.random.split(block_key, 3)
        others = jnp.arange((DEVICES - 1) * CAP, dtype=jnp.int32) // CAP
        others = others + (others >= hot_owner).astype(jnp.int32)
        picked = jax.random.permutation(first, others)[:TOK_DEV - CAP]
        owners = jnp.concatenate([jnp.full((CAP,), hot_owner, jnp.int32), picked])
        local = jax.random.randint(second, (TOK_DEV,), 0, EXP_DEV)
        return jax.random.permutation(third, owners * EXP_DEV + local)
    block_keys = jax.random.split(jax.random.fold_in(key, 23), N_STORE * N_SEQ)
    blocks = jax.vmap(one_block)(block_keys)
    return blocks.reshape(N_STORE, LENGTH).astype(jnp.int32)


def levels(key, shape, cuts, smallest, high):
    factor_of = 1.0
    for position, blocks in cuts:
        heights = jax.random.uniform(jax.random.fold_in(jax.random.fold_in(key, 6), position), (blocks,), jnp.float32, smallest / len(cuts), high / len(cuts))
        factor_of = factor_of * jnp.repeat(jnp.exp(heights), shape[position] // blocks).reshape((-1,) + (1,) * (len(shape) - 1 - position))
    return factor_of


def split_up(count, total, bound, lean):
    portions = [(1 << 20) // math.isqrt(rank ** lean) + 1 for rank in range(2, count + 1)]
    rest, given = total - bound - (count - 1), [1] * (count - 1)
    while rest > 0:
        candidates = [i for i in range(count - 1) if given[i] < bound]
        whole, budget = sum([portions[i] for i in candidates]), rest
        for i in candidates:
            addition = min(bound - given[i], max(1, budget * portions[i] // whole), rest)
            given[i] = given[i] + addition
            rest = rest - addition
    return np.array([bound] + given)


def ragged(own_key, amount, total, limit, lean):
    if amount == 2:
        one = jax.random.randint(own_key, (), max(1, total - limit), min(limit, total - 1) + 1)
        return jnp.stack([one, total - one])
    tallies = jnp.asarray(split_up(amount, total, limit, lean), jnp.int32)
    pairs = (amount - 1) // 2
    source_of, sink = tallies[1:1 + 2 * pairs:2], tallies[2:2 + 2 * pairs:2]
    slack = jnp.minimum(source_of - 1, limit - sink)
    passed = jax.random.randint(jax.random.fold_in(own_key, 1), (pairs,), 0, 1 << 20) % (slack + 1)
    tallies = tallies.at[1:1 + 2 * pairs:2].set(source_of - passed).at[2:2 + 2 * pairs:2].set(sink + passed)
    return tallies[jax.random.permutation(jax.random.fold_in(own_key, 2), amount)]


def normal_values(own_key, dims, spread, most, cuts=(), kind=jnp.bfloat16):
    array = spread * jax.random.normal(own_key, dims, jnp.float32)
    if cuts:
        array = array * levels(own_key, dims, cuts, -0.22, 0.18)
    return jnp.clip(array, -most, most).astype(kind)


def setup_inputs(seed: int = 0) -> dict:
    splits = jax.random.split(jax.random.key(seed), 8)
    return {
        "queries": draw_queries(jax.random.fold_in(splits[7], 71), 0),
        "keys": draw_keys(jax.random.fold_in(splits[7], 71), 0),
        "values": normal_values(splits[2], (N_STORE, LENGTH, KV_HEADS * HEAD_DIM), 1.0, 6.0, ((0, 2), (1, 16))),
        "segment_ids": jax.vmap(lambda own: jnp.searchsorted(jnp.cumsum(ragged(own, 4, LENGTH, LENGTH // 2, 0)), jnp.arange(LENGTH), side="right"))(jax.random.split(splits[3], N_STORE)).reshape((N_STORE, LENGTH)).astype(jnp.int32),
        "route_ids": draw_route_ids(jax.random.fold_in(splits[7], 71), 0),
        "adapter_down": normal_values(splits[5], (WIDTH, EXPERTS * RANK), WIDTH ** -0.5, 0.09375, ((1, 32),)),
        "adapter_up": normal_values(splits[6], (EXPERTS * RANK, WIDTH), RANK ** -0.5, 0.75, ((0, 32),)),
    }


def attend_one(queries, keys, values, segments):
    length = queries.shape[0]
    group = HEADS // KV_HEADS
    block = min(512, length)
    q_four = queries.reshape(length, KV_HEADS, group, HEAD_DIM)
    k_float = keys.reshape(length, KV_HEADS, HEAD_DIM).astype(jnp.float32)
    v_float = values.reshape(length, KV_HEADS, HEAD_DIM).astype(jnp.float32)
    key_pos = jnp.arange(length, dtype=jnp.int32)
    scale = HEAD_DIM ** -0.5

    def one_block(index):
        start = (index * block).astype(jnp.int32)
        q_block = lax.dynamic_slice_in_dim(q_four, start, block, 0).astype(jnp.float32)
        seg_block = lax.dynamic_slice_in_dim(segments, start, block, 0)
        scores = jnp.einsum('qkgd,nkd->kgqn', q_block, k_float) * scale
        q_pos = start + jnp.arange(block, dtype=jnp.int32)
        allowed = (key_pos[None, :] <= q_pos[:, None]) & (segments[None, :] == seg_block[:, None])
        scores = jnp.where(allowed[None, None], scores, jnp.float32(-1e30))
        top = jnp.max(scores, axis=-1, keepdims=True)
        expo = jnp.exp(scores - top)
        total = jnp.sum(expo, axis=-1)
        weights = expo.astype(jnp.bfloat16).astype(jnp.float32)
        summed = jnp.einsum('kgqn,nkd->qkgd', weights, v_float)
        out = summed / jnp.transpose(total, (2, 0, 1))[:, :, :, None]
        return out.astype(jnp.bfloat16).reshape(block, HEADS * HEAD_DIM)

    blocks = lax.map(one_block, jnp.arange(length // block, dtype=jnp.int32))
    return blocks.reshape(length, HEADS * HEAD_DIM)


def reference(queries, keys, values, segment_ids, route_ids, adapter_down, adapter_up):
    contexts = []
    for index in range(N_STORE):
        contexts.append(attend_one(queries[index], keys[index], values[index], segment_ids[index]))
    context = jnp.stack(contexts).reshape(-1, WIDTH)
    route = route_ids.reshape(-1)
    down_three = adapter_down.reshape(WIDTH, EXPERTS, RANK)
    up_three = adapter_up.reshape(EXPERTS, RANK, WIDTH)
    rows_block = 64

    def one_rows(index):
        start = (index * rows_block).astype(jnp.int32)
        x_rows = lax.dynamic_slice_in_dim(context, start, rows_block, 0).astype(jnp.float32)
        chosen = lax.dynamic_slice_in_dim(route, start, rows_block, 0)
        down_rows = jnp.take(down_three, chosen, axis=1).astype(jnp.float32)
        low = jnp.einsum('tw,wtr->tr', x_rows, down_rows).astype(jnp.bfloat16)
        up_rows = jnp.take(up_three, chosen, axis=0).astype(jnp.float32)
        delta = jnp.einsum('tr,trw->tw', low.astype(jnp.float32), up_rows).astype(jnp.bfloat16)
        return (x_rows + delta.astype(jnp.float32)).astype(jnp.bfloat16)

    mixed = lax.map(one_rows, jnp.arange(context.shape[0] // rows_block, dtype=jnp.int32))
    return mixed.reshape(N_STORE, LENGTH, WIDTH)
```

```python
import functools

import jax
import jax.numpy as jnp
from jax import lax
from jax.experimental import pallas as pl
from jax.experimental.pallas import tpu as pltpu
from jax.sharding import PartitionSpec as P

HEAD_DIM = 128
HEADS = 32
KV_HEADS = 4
RANK = 64
EXP_DEV = 16
GROUPS = 4
HOPS = 2
SEG_ROWS = 16
MESH = pl.DeviceIdType.MESH


def gather_kernel(n_seq, own_ref, out_ref, local_sem, send_sem, recv_sem):
    per = n_seq // GROUPS
    me = lax.axis_index("seq")
    st = lax.axis_index("store")
    level = me // per
    bits = []
    bit = 2
    while bit < per:
        bits.append(bit)
        bit *= 2
    bits.append(1)

    def flip(b, index=None):
        index = me if index is None else index
        return index + b - 2 * b * ((index // b) % 2)

    barrier = pltpu.get_barrier_semaphore()
    for b in bits:
        pl.semaphore_signal(barrier, inc=1, device_id=(flip(b), st), device_id_type=MESH)

    @pl.when(level < GROUPS - 1)
    def _():
        pl.semaphore_signal(barrier, inc=1, device_id=(me + per, st), device_id_type=MESH)

    @pl.when(level > 0)
    def _():
        pl.semaphore_signal(barrier, inc=1, device_id=(me - per, st), device_id_type=MESH)

    ends = (level < GROUPS - 1).astype(jnp.int32) + (level > 0).astype(jnp.int32)
    pl.semaphore_wait(barrier, len(bits) + ends)

    def remote(source, block, target, sem):
        return pltpu.make_async_remote_copy(
            src_ref=source,
            dst_ref=out_ref.at[block],
            send_sem=send_sem.at[sem],
            recv_sem=recv_sem.at[sem],
            device_id=(target, st),
            device_id_type=MESH,
        )

    def guarded(condition, act):
        if condition is None:
            act()
        else:
            pl.when(condition)(act)

    steps = []
    sem = HOPS
    for hop in range(HOPS + 1):
        masks = [0]
        for b in bits:
            for m in masks:
                steps.append((sem, m, hop, b))
                sem += 1
            masks = masks + [m ^ b for m in masks]

    def column(m):
        index = me
        for b in bits:
            if m & b:
                index = flip(b, index)
        return index

    def at(m, hop):
        return jnp.maximum(column(m) - hop * per, 0)

    def block_ref(m, hop):
        return own_ref if (m == 0 and hop == 0) else out_ref.at[at(m, hop)]

    mine = pltpu.make_async_copy(own_ref, out_ref.at[me], local_sem)
    mine.start()
    up = jnp.minimum(me + per, n_seq - 1)

    def z_copy(hop):
        return remote(block_ref(0, hop), at(0, hop), up, hop)

    def z_arrival(hop):
        return remote(block_ref(0, hop), at(0, hop), up, hop - 1)

    def x_copy(step):
        s, m, hop, b = step
        return remote(block_ref(m, hop), at(m, hop), flip(b), s)

    def x_arrival(step):
        s, m, hop, b = step
        ref = out_ref.at[jnp.maximum(flip(b, column(m)) - hop * per, 0)]
        return pltpu.make_async_remote_copy(
            src_ref=ref, dst_ref=ref, send_sem=send_sem.at[s], recv_sem=recv_sem.at[s],
            device_id=(flip(b), st), device_id_type=MESH,
        )

    z_conditions = [(level < GROUPS - 1) & (level >= hop) for hop in range(HOPS)]
    guarded(z_conditions[0], lambda: z_copy(0).start())
    for hop in range(HOPS + 1):
        condition = None if hop == 0 else level >= hop
        if hop > 0:
            arrived = z_arrival(hop)
            guarded(condition, arrived.wait_recv)
            if hop < HOPS:
                guarded(z_conditions[hop], z_copy(hop).start)
        group = [s for s in steps if s[2] == hop]

        first = [s for s in group if s[1] == 0]

        def begin(first=first):
            for s in first:
                x_copy(s).start()

        guarded(condition, begin)
    for hop in range(HOPS + 1):
        condition = None if hop == 0 else level >= hop
        group = [s for s in steps if s[2] == hop]

        def rest(group=group):
            have = {0}
            waiting = list(group)
            for position, b in enumerate(bits):
                stage = [s for s in waiting if s[3] == b]
                for s in stage:
                    if s[1] != 0:
                        x_copy(s).start()
                for s in stage:
                    x_arrival(s).wait_recv()
            for s in group:
                x_copy(s).wait_send()

        guarded(condition, rest)
    for hop in range(HOPS):
        guarded(z_conditions[hop], z_copy(hop).wait_send)
    mine.wait()


def gather_blocks(block, n_seq):
    per = n_seq // GROUPS
    copies = HOPS + (HOPS + 1) * (per - 1)
    return pl.pallas_call(
        functools.partial(gather_kernel, n_seq),
        out_shape=jax.ShapeDtypeStruct((n_seq,) + block.shape, block.dtype),
        in_specs=[pl.BlockSpec(memory_space=pl.ANY)],
        out_specs=pl.BlockSpec(memory_space=pl.ANY),
        scratch_shapes=[
            pltpu.SemaphoreType.DMA,
            pltpu.SemaphoreType.DMA((copies,)),
            pltpu.SemaphoreType.DMA((copies,)),
        ],
        compiler_params=pltpu.CompilerParams(collective_id=1, has_side_effects=True),
        name="gather_blocks",
    )(block)


def attend_kernel(tok, info_ref, q_ref, k_ref, v_ref, kseg_ref, qseg_ref, place_ref, ctx_ref, send_ref, m_ref, l_ref, acc_ref):
    group = HEADS // KV_HEADS
    me = info_ref[0]
    first = info_ref[1]
    coef = (HEAD_DIM**-0.5) * 1.4426950408889634
    q = jnp.concatenate([q_ref[:, h * HEAD_DIM : (h + 1) * HEAD_DIM] for h in range(group)], axis=0)
    m_ref[...] = jnp.full_like(m_ref, -1e30)
    l_ref[...] = jnp.zeros_like(l_ref)
    acc_ref[...] = jnp.zeros_like(acc_ref)

    @pl.loop(first // 2, me // 2 + 1)
    def _(pair):
        k = k_ref[pl.ds(2 * pair, 2), :tok].reshape(2 * tok, HEAD_DIM)
        v = v_ref[pl.ds(2 * pair, 2), :tok].reshape(2 * tok, HEAD_DIM)
        s = lax.dot_general(k, q, (((1,), (1,)), ((), ())), preferred_element_type=jnp.float32)
        key_pos = 2 * pair * tok + lax.broadcasted_iota(jnp.int32, (2 * tok, tok), 0)
        q_pos = me * tok + lax.broadcasted_iota(jnp.int32, (2 * tok, tok), 1)
        kseg = kseg_ref[pl.ds(2 * pair, 2)].reshape(2 * tok, 1)
        seen = (key_pos <= q_pos) & (kseg == qseg_ref[...])
        bias = jnp.where(seen, 0.0, -1e30).astype(jnp.float32)
        s = s + jnp.concatenate([bias] * group, axis=1)
        m_old = m_ref[...]
        m_new = jnp.maximum(m_old, jnp.max(s, axis=0, keepdims=True))
        alpha = jnp.exp2((m_old - m_new) * coef)
        p = jnp.exp2((s - m_new) * coef)
        m_ref[...] = m_new
        l_ref[...] = l_ref[...] * alpha + jnp.sum(p, axis=0, keepdims=True)
        pv = lax.dot_general(
            v, p.astype(jnp.bfloat16), (((0,), (0,)), ((), ())), preferred_element_type=jnp.float32
        )
        acc_ref[...] = acc_ref[...] * alpha + pv

    out = acc_ref[...] / l_ref[...]
    for h in range(group):
        ctx_ref[:, h * HEAD_DIM : (h + 1) * HEAD_DIM] = out[:, h * tok : (h + 1) * tok].T.astype(jnp.bfloat16)
    send_ref[...] = jnp.dot(place_ref[...], ctx_ref[...], preferred_element_type=jnp.float32).astype(jnp.bfloat16)


def attend(info, queries, blocks, kseg, qseg, place):
    tok, width = queries.shape
    n_seq, rows, _ = blocks.shape
    slots = place.shape[0]
    part = width // KV_HEADS
    cols = tok * (HEADS // KV_HEADS)
    return pl.pallas_call(
        functools.partial(attend_kernel, tok),
        out_shape=(
            jax.ShapeDtypeStruct((tok, width), jnp.bfloat16),
            jax.ShapeDtypeStruct((slots, width), jnp.bfloat16),
        ),
        grid=(KV_HEADS,),
        in_specs=[
            pl.BlockSpec(memory_space=pltpu.SMEM),
            pl.BlockSpec((tok, part), lambda g: (0, g)),
            pl.BlockSpec((n_seq, rows, HEAD_DIM), lambda g: (0, 0, g)),
            pl.BlockSpec((n_seq, rows, HEAD_DIM), lambda g: (0, 0, KV_HEADS + g)),
            pl.BlockSpec((n_seq, tok, 1), lambda g: (0, 0, 0)),
            pl.BlockSpec((1, tok), lambda g: (0, 0)),
            pl.BlockSpec((slots, tok), lambda g: (0, 0)),
        ],
        out_specs=(
            pl.BlockSpec((tok, part), lambda g: (0, g)),
            pl.BlockSpec((slots, part), lambda g: (0, g)),
        ),
        scratch_shapes=[
            pltpu.VMEM((1, cols), jnp.float32),
            pltpu.VMEM((1, cols), jnp.float32),
            pltpu.VMEM((HEAD_DIM, cols), jnp.float32),
        ],
        compiler_params=pltpu.CompilerParams(vmem_limit_bytes=48 << 20),
        name="attend",
    )(info, queries, blocks, blocks, kseg, qseg, place)


def local(queries, keys, values, segment_ids, route_ids, adapter_down, adapter_up):
    n_seq = lax.axis_size("seq")
    n_store = lax.axis_size("store")
    tok = queries.shape[1]
    width = queries.shape[2]
    me = lax.axis_index("seq")
    seg = segment_ids[0].astype(jnp.bfloat16)
    seg_row = jnp.pad(seg[None, :], ((0, SEG_ROWS - 1), (0, keys.shape[2] * 2 - tok)))
    own = jnp.concatenate([jnp.concatenate([keys[0], values[0]], axis=1), seg_row], axis=0)
    blocks = gather_blocks(own, n_seq)

    devices = n_seq * n_store
    capacity = max(2, 2 * tok // devices)
    chosen = route_ids[0]
    owners = chosen // EXP_DEV
    one_hot = (owners[:, None] == jnp.arange(devices, dtype=jnp.int32)[None, :]).astype(jnp.bfloat16)
    lower = jnp.tril(jnp.ones((tok, tok), jnp.bfloat16))
    counts = jnp.dot(lower, one_hot, preferred_element_type=jnp.float32)
    slot_of = jnp.sum(counts * one_hot.astype(jnp.float32), axis=1).astype(jnp.int32) - 1
    placed = owners * capacity + slot_of
    hits = jnp.arange(devices * capacity, dtype=jnp.int32)[:, None] == placed[None, :]
    place = hits.astype(jnp.bfloat16)
    send_tags = (
        jnp.sum(jnp.where(hits, (chosen % EXP_DEV + 1).astype(jnp.float32)[None, :], 0.0), axis=1) - 1.0
    ).astype(jnp.bfloat16)
    tags = lax.all_to_all(
        send_tags.reshape(devices, capacity), ("seq", "store"), split_axis=0, concat_axis=0, tiled=True
    ).reshape(-1, 1)

    kseg = blocks[:, tok, :tok].astype(jnp.float32)
    qseg = seg.astype(jnp.float32)
    index = jnp.arange(n_seq, dtype=jnp.int32)
    wanted = (index >= me - n_seq // HOPS) & (index < me) & (kseg[:, tok - 1] >= qseg[0])
    first = jnp.min(jnp.where(wanted, index, me))
    info = jnp.stack([me, first]).astype(jnp.int32)
    tok_ctx, send_rows = attend(info, queries[0], blocks, kseg[:, :, None], qseg[None, :], place)

    flat_rows = lax.all_to_all(
        send_rows.reshape(devices, capacity, width), ("seq", "store"), split_axis=0, concat_axis=0, tiled=True
    ).reshape(-1, width)
    low = jnp.dot(flat_rows, adapter_down, preferred_element_type=jnp.float32)
    lane_owner = (jnp.arange(low.shape[1], dtype=jnp.int32) // RANK).astype(jnp.float32)
    low = jnp.where(tags.astype(jnp.float32) == lane_owner[None, :], low, 0.0).astype(jnp.bfloat16)
    delta = jnp.dot(low, adapter_up, preferred_element_type=jnp.float32).astype(jnp.bfloat16)
    answer = lax.all_to_all(
        delta.reshape(devices, capacity, width), ("seq", "store"), split_axis=0, concat_axis=0, tiled=True
    ).reshape(-1, width)
    delta_rows = lax.dot_general(place, answer, (((0,), (0,)), ((), ())), preferred_element_type=jnp.float32)
    return (tok_ctx.astype(jnp.float32) + delta_rows).astype(jnp.bfloat16)[None]


def solution(mesh):
    return jax.shard_map(
        local,
        mesh=mesh,
        in_specs=(
            P("store", "seq", None),
            P("store", "seq", None),
            P("store", "seq", None),
            P("store", "seq"),
            P("store", "seq"),
            P(None, ("seq", "store")),
            P(("seq", "store"), None),
        ),
        out_specs=P("store", "seq", None),
        check_vma=False,
    )
```

```python
import functools

import jax
import jax.numpy as jnp
from jax import lax
from jax.experimental import pallas as pl
from jax.experimental.pallas import tpu as pltpu
from jax.sharding import PartitionSpec as P

HEAD_DIM = 128
HEADS = 32
KV_HEADS = 4
RANK = 64
EXP_DEV = 16
GROUPS = 4
HOPS = 2
SEG_ROWS = 16
MESH = pl.DeviceIdType.MESH


def gather_kernel(n_seq, own_ref, out_ref, local_sem, send_sem, recv_sem):
    per = n_seq // GROUPS
    me = lax.axis_index("seq")
    st = lax.axis_index("store")
    level = me // per
    bits = []
    bit = 2
    while bit < per:
        bits.append(bit)
        bit *= 2
    bits.append(1)

    def flip(b, index=None):
        index = me if index is None else index
        return index + b - 2 * b * ((index // b) % 2)

    barrier = pltpu.get_barrier_semaphore()
    for b in bits:
        pl.semaphore_signal(barrier, inc=1, device_id=(flip(b), st), device_id_type=MESH)

    @pl.when(level < GROUPS - 1)
    def _():
        pl.semaphore_signal(barrier, inc=1, device_id=(me + per, st), device_id_type=MESH)

    @pl.when(level > 0)
    def _():
        pl.semaphore_signal(barrier, inc=1, device_id=(me - per, st), device_id_type=MESH)

    ends = (level < GROUPS - 1).astype(jnp.int32) + (level > 0).astype(jnp.int32)
    pl.semaphore_wait(barrier, len(bits) + ends)

    def remote(source, block, target, sem):
        return pltpu.make_async_remote_copy(
            src_ref=source,
            dst_ref=out_ref.at[block],
            send_sem=send_sem.at[sem],
            recv_sem=recv_sem.at[sem],
            device_id=(target, st),
            device_id_type=MESH,
        )

    def guarded(condition, act):
        if condition is None:
            act()
        else:
            pl.when(condition)(act)

    steps = []
    sem = HOPS
    for hop in range(HOPS + 1):
        masks = [0]
        for b in bits:
            for m in masks:
                steps.append((sem, m, hop, b))
                sem += 1
            masks = masks + [m ^ b for m in masks]

    def column(m):
        index = me
        for b in bits:
            if m & b:
                index = flip(b, index)
        return index

    def at(m, hop):
        return jnp.maximum(column(m) - hop * per, 0)

    def block_ref(m, hop):
        return own_ref if (m == 0 and hop == 0) else out_ref.at[at(m, hop)]

    mine = pltpu.make_async_copy(own_ref, out_ref.at[me], local_sem)
    mine.start()
    up = jnp.minimum(me + per, n_seq - 1)

    def z_copy(hop):
        return remote(block_ref(0, hop), at(0, hop), up, hop)

    def z_arrival(hop):
        return remote(block_ref(0, hop), at(0, hop), up, hop - 1)

    def x_copy(step):
        s, m, hop, b = step
        return remote(block_ref(m, hop), at(m, hop), flip(b), s)

    def x_arrival(step):
        s, m, hop, b = step
        ref = out_ref.at[jnp.maximum(flip(b, column(m)) - hop * per, 0)]
        return pltpu.make_async_remote_copy(
            src_ref=ref, dst_ref=ref, send_sem=send_sem.at[s], recv_sem=recv_sem.at[s],
            device_id=(flip(b), st), device_id_type=MESH,
        )

    z_conditions = [(level < GROUPS - 1) & (level >= hop) for hop in range(HOPS)]
    guarded(z_conditions[0], lambda: z_copy(0).start())
    for hop in range(HOPS + 1):
        condition = None if hop == 0 else level >= hop
        if hop > 0:
            arrived = z_arrival(hop)
            guarded(condition, arrived.wait_recv)
            if hop < HOPS:
                guarded(z_conditions[hop], z_copy(hop).start)
        group = [s for s in steps if s[2] == hop]

        first = [s for s in group if s[1] == 0]

        def begin(first=first):
            for s in first:
                x_copy(s).start()

        guarded(condition, begin)
    for hop in range(HOPS + 1):
        condition = None if hop == 0 else level >= hop
        group = [s for s in steps if s[2] == hop]

        def rest(group=group):
            have = {0}
            waiting = list(group)
            for position, b in enumerate(bits):
                stage = [s for s in waiting if s[3] == b]
                for s in stage:
                    if s[1] != 0:
                        x_copy(s).start()
                for s in stage:
                    x_arrival(s).wait_recv()
            for s in group:
                x_copy(s).wait_send()

        guarded(condition, rest)
    for hop in range(HOPS):
        guarded(z_conditions[hop], z_copy(hop).wait_send)
    mine.wait()


def gather_blocks(block, n_seq):
    per = n_seq // GROUPS
    copies = HOPS + (HOPS + 1) * (per - 1)
    return pl.pallas_call(
        functools.partial(gather_kernel, n_seq),
        out_shape=jax.ShapeDtypeStruct((n_seq,) + block.shape, block.dtype),
        in_specs=[pl.BlockSpec(memory_space=pl.ANY)],
        out_specs=pl.BlockSpec(memory_space=pl.ANY),
        scratch_shapes=[
            pltpu.SemaphoreType.DMA,
            pltpu.SemaphoreType.DMA((copies,)),
            pltpu.SemaphoreType.DMA((copies,)),
        ],
        compiler_params=pltpu.CompilerParams(collective_id=1, has_side_effects=True),
        name="gather_blocks",
    )(block)


def routed_kernel(
    n_store, devices, cap,
    q_ref, kv_ref, kseg_ref, qseg_ref, place_ref, tags_ref, down_hbm, up_hbm,
    out_ref,
    weight_ref, ctx_ref, m_ref, l_ref, acc_ref, send_ref, got_ref, ans_ref, tag_ref, total_ref, low_ref,
    load_sem, send_sem, recv_sem,
):
    tok = q_ref.shape[0]
    n_seq = kv_ref.shape[0]
    group = HEADS // KV_HEADS
    part = group * HEAD_DIM
    split = SEG_ROWS // cap
    piece = part // split
    slots = devices * cap
    packed = devices * SEG_ROWS
    me = lax.axis_index("seq")
    flat = me * n_store + lax.axis_index("store")
    coef = (HEAD_DIM**-0.5) * 1.4426950408889634

    up_at = weight_ref.shape[0] - 1

    def load_down(g):
        rows = pl.ds(pl.multiple_of(g * part, part), part)
        return pltpu.make_async_copy(down_hbm.at[rows], weight_ref.at[0, g], load_sem.at[g])

    def load_up(g):
        cols = pl.ds(pl.multiple_of(g * part, part), part)
        return pltpu.make_async_copy(up_hbm.at[:, cols], weight_ref.at[up_at, g], load_sem.at[KV_HEADS + g])

    @pl.loop(0, KV_HEADS)
    def _(g):
        load_down(g).start()
        if up_at:
            load_up(g).start()

    barrier = pltpu.get_barrier_semaphore()

    @pl.loop(1, devices)
    def _(p):
        peer = (flat + p) % devices
        pl.semaphore_signal(barrier, inc=1, device_id=(peer // n_store, peer % n_store), device_id_type=MESH)

    pl.semaphore_wait(barrier, devices - 1)

    def exchange(source, target, sem):
        @pl.loop(1, devices)
        def _(p):
            peer = (flat + p) % devices
            pltpu.make_async_remote_copy(
                src_ref=source.at[peer], dst_ref=target.at[flat], send_sem=send_sem.at[sem], recv_sem=recv_sem.at[sem],
                device_id=(peer // n_store, peer % n_store), device_id_type=MESH,
            ).start()

    def all_of(source, target, sem):
        others = pl.ds(0, devices - 1)
        return pltpu.make_async_remote_copy(
            src_ref=source.at[others], dst_ref=target.at[others], send_sem=send_sem.at[sem], recv_sem=recv_sem.at[sem],
            device_id=((me + 1) % n_seq, lax.axis_index("store")), device_id_type=MESH,
        )

    exchange(tags_ref, tag_ref, 2 * KV_HEADS)
    tag_ref[flat] = tags_ref[flat]

    @pl.loop(0, KV_HEADS)
    def _(g):
        start = pl.multiple_of(g * part, part)
        q_all = q_ref[:, pl.ds(start, part)]
        q = jnp.concatenate([q_all[:, h * HEAD_DIM : (h + 1) * HEAD_DIM] for h in range(group)], axis=0)
        m_ref[...] = jnp.full_like(m_ref, -1e30)
        l_ref[...] = jnp.zeros_like(l_ref)
        acc_ref[...] = jnp.zeros_like(acc_ref)
        k_cols = pl.ds(pl.multiple_of(g * HEAD_DIM, HEAD_DIM), HEAD_DIM)
        v_cols = pl.ds(pl.multiple_of((KV_HEADS + g) * HEAD_DIM, HEAD_DIM), HEAD_DIM)

        @pl.loop(jnp.maximum(me - n_seq // HOPS, 0) // 2, me // 2 + 1)
        def _(pair):
            k = kv_ref[pl.ds(2 * pair, 2), :tok, k_cols].reshape(2 * tok, HEAD_DIM)
            v = kv_ref[pl.ds(2 * pair, 2), :tok, v_cols].reshape(2 * tok, HEAD_DIM)
            s = lax.dot_general(k, q, (((1,), (1,)), ((), ())), preferred_element_type=jnp.float32)
            key_pos = 2 * pair * tok + lax.broadcasted_iota(jnp.int32, (2 * tok, tok), 0)
            q_pos = me * tok + lax.broadcasted_iota(jnp.int32, (2 * tok, tok), 1)
            kseg = kseg_ref[pl.ds(2 * pair, 2)].reshape(2 * tok, 1)
            seen = (key_pos <= q_pos) & (kseg == qseg_ref[...])
            bias = jnp.where(seen, 0.0, -1e30).astype(jnp.float32)
            s = s + jnp.concatenate([bias] * group, axis=1)
            m_old = m_ref[...]
            m_new = jnp.maximum(m_old, jnp.max(s, axis=0, keepdims=True))
            alpha = jnp.exp2((m_old - m_new) * coef)
            p = jnp.exp2((s - m_new) * coef)
            m_ref[...] = m_new
            l_ref[...] = l_ref[...] * alpha + jnp.sum(p, axis=0, keepdims=True)
            pv = lax.dot_general(
                v, p.astype(jnp.bfloat16), (((0,), (0,)), ((), ())), preferred_element_type=jnp.float32
            )
            acc_ref[...] = acc_ref[...] * alpha + pv

        out = acc_ref[...] / l_ref[...]
        ctx = jnp.concatenate([out[:, h * tok : (h + 1) * tok].T for h in range(group)], axis=1).astype(jnp.bfloat16)
        ctx_ref[:, pl.ds(start, part)] = ctx
        stacked = jnp.concatenate([ctx[:, i * piece : (i + 1) * piece] for i in range(split)], axis=0)
        rows = jnp.dot(place_ref[...], stacked, preferred_element_type=jnp.float32).astype(jnp.bfloat16)
        send_ref[g] = rows.reshape(devices, SEG_ROWS, piece)
        exchange(send_ref.at[g], got_ref.at[g], g)
        got_ref[g, flat] = send_ref[g, flat]

    def chosen_rows(i):
        row = lax.broadcasted_iota(jnp.int32, (slots, 1), 0)
        column = lax.broadcasted_iota(jnp.int32, (1, packed), 1)
        wanted = (row // cap) * SEG_ROWS + i * cap + row % cap
        return jnp.where(column == wanted, 1.0, 0.0).astype(jnp.bfloat16)

    total_ref[...] = jnp.zeros_like(total_ref)
    all_of(tags_ref, tag_ref, 2 * KV_HEADS).wait()

    @pl.loop(0, KV_HEADS)
    def _(g):
        all_of(send_ref.at[g], got_ref.at[g], g).wait_recv()
        load_down(g).wait()
        got = got_ref[g].reshape(packed, piece)
        for i in range(split):
            rows = jnp.dot(chosen_rows(i), got, preferred_element_type=jnp.float32).astype(jnp.bfloat16)
            total_ref[...] += jnp.dot(rows, weight_ref[0, g, pl.ds(i * piece, piece)], preferred_element_type=jnp.float32)

    tags = jnp.dot(chosen_rows(0), tag_ref[...].reshape(packed, HEAD_DIM), preferred_element_type=jnp.float32)
    held = total_ref.shape[1]
    lane = lax.broadcasted_iota(jnp.int32, (slots, held), 1) // RANK + 1
    tags = jnp.concatenate([tags] * (held // HEAD_DIM), axis=1)
    low_ref[...] = jnp.where(tags == lane.astype(jnp.float32), total_ref[...], 0.0).astype(jnp.bfloat16)
    if not up_at:

        @pl.loop(0, KV_HEADS)
        def _(g):
            load_up(g).start()

    @pl.loop(0, KV_HEADS)
    def _(g):
        load_up(g).wait()
        delta = jnp.dot(low_ref[...], weight_ref[up_at, g], preferred_element_type=jnp.float32).astype(jnp.bfloat16)
        rows = jnp.zeros((packed, piece), jnp.float32)
        for i in range(split):
            rows += lax.dot_general(
                chosen_rows(i), delta[:, i * piece : (i + 1) * piece], (((0,), (0,)), ((), ())),
                preferred_element_type=jnp.float32,
            )
        all_of(send_ref.at[g], got_ref.at[g], g).wait_send()
        send_ref[g] = rows.astype(jnp.bfloat16).reshape(devices, SEG_ROWS, piece)
        exchange(send_ref.at[g], ans_ref.at[g], KV_HEADS + g)
        ans_ref[g, flat] = send_ref[g, flat]

    @pl.loop(0, KV_HEADS)
    def _(g):
        all_of(send_ref.at[g], ans_ref.at[g], KV_HEADS + g).wait_recv()
        rows = ans_ref[g].reshape(packed, piece)
        delta = jnp.concatenate(
            [
                lax.dot_general(
                    place_ref[:, i * tok : (i + 1) * tok], rows, (((0,), (0,)), ((), ())),
                    preferred_element_type=jnp.float32,
                )
                for i in range(split)
            ],
            axis=1,
        )
        cols = pl.ds(pl.multiple_of(g * part, part), part)
        out_ref[:, cols] = (ctx_ref[:, cols].astype(jnp.float32) + delta).astype(jnp.bfloat16)

    @pl.loop(0, KV_HEADS)
    def _(g):
        all_of(send_ref.at[g], ans_ref.at[g], KV_HEADS + g).wait_send()


def routed(n_store, devices, cap, queries, blocks, kseg, qseg, place, tags, down, up):
    tok, width = queries.shape
    part = width // KV_HEADS
    held = down.shape[1]
    cols = tok * (HEADS // KV_HEADS)
    wire = (KV_HEADS, devices, SEG_ROWS, part * cap // SEG_ROWS)
    vmem = pl.BlockSpec(memory_space=pltpu.VMEM)
    hbm = pl.BlockSpec(memory_space=pl.ANY)
    return pl.pallas_call(
        functools.partial(routed_kernel, n_store, devices, cap),
        out_shape=jax.ShapeDtypeStruct((tok, width), jnp.bfloat16),
        in_specs=[vmem] * 6 + [hbm] * 2,
        out_specs=vmem,
        scratch_shapes=[
            pltpu.VMEM((2 if devices <= 32 else 1, KV_HEADS, part, held), jnp.bfloat16),
            pltpu.VMEM((tok, width), jnp.bfloat16),
            pltpu.VMEM((1, cols), jnp.float32),
            pltpu.VMEM((1, cols), jnp.float32),
            pltpu.VMEM((HEAD_DIM, cols), jnp.float32),
            pltpu.VMEM(wire, jnp.bfloat16),
            pltpu.VMEM(wire, jnp.bfloat16),
            pltpu.VMEM(wire, jnp.bfloat16),
            pltpu.VMEM(tags.shape, jnp.bfloat16),
            pltpu.VMEM((devices * cap, held), jnp.float32),
            pltpu.VMEM((devices * cap, held), jnp.bfloat16),
            pltpu.SemaphoreType.DMA((2 * KV_HEADS,)),
            pltpu.SemaphoreType.DMA((2 * KV_HEADS + 1,)),
            pltpu.SemaphoreType.DMA((2 * KV_HEADS + 1,)),
        ],
        compiler_params=pltpu.CompilerParams(collective_id=2, has_side_effects=True, vmem_limit_bytes=62 << 20),
        name="routed",
    )(queries, blocks, kseg, qseg, place, tags, down, up)


def local(queries, keys, values, segment_ids, route_ids, adapter_down, adapter_up):
    n_seq = lax.axis_size("seq")
    n_store = lax.axis_size("store")
    tok = queries.shape[1]
    seg = segment_ids[0].astype(jnp.bfloat16)
    seg_row = jnp.pad(seg[None, :], ((0, SEG_ROWS - 1), (0, keys.shape[2] * 2 - tok)))
    own = jnp.concatenate([jnp.concatenate([keys[0], values[0]], axis=1), seg_row], axis=0)
    blocks = gather_blocks(own, n_seq)

    devices = n_seq * n_store
    capacity = max(2, 2 * tok // devices)
    split = SEG_ROWS // capacity
    chosen = route_ids[0]
    owners = chosen // EXP_DEV
    one_hot = (owners[:, None] == jnp.arange(devices, dtype=jnp.int32)[None, :]).astype(jnp.bfloat16)
    lower = jnp.tril(jnp.ones((tok, tok), jnp.bfloat16))
    counts = jnp.dot(lower, one_hot, preferred_element_type=jnp.float32)
    slot_of = jnp.sum(counts * one_hot.astype(jnp.float32), axis=1).astype(jnp.int32) - 1
    placed = owners * SEG_ROWS + slot_of
    packed = jnp.arange(devices * SEG_ROWS, dtype=jnp.int32)[:, None]
    place = (packed == jnp.concatenate([placed + i * capacity for i in range(split)])[None, :]).astype(jnp.bfloat16)
    names = (chosen % EXP_DEV + 1).astype(jnp.bfloat16)
    tags = jnp.dot(
        place[:, :tok], jnp.broadcast_to(names[:, None], (tok, HEAD_DIM)), preferred_element_type=jnp.float32
    ).astype(jnp.bfloat16)
    tags = tags.reshape(devices, SEG_ROWS, HEAD_DIM)

    kseg = blocks[:, tok, :tok].astype(jnp.float32)[:, :, None]
    qseg = seg.astype(jnp.float32)[None, :]
    return routed(
        n_store, devices, capacity, queries[0], blocks, kseg, qseg, place, tags, adapter_down, adapter_up
    )[None]


def solution(mesh):
    return jax.shard_map(
        local,
        mesh=mesh,
        in_specs=(
            P("store", "seq", None),
            P("store", "seq", None),
            P("store", "seq", None),
            P("store", "seq"),
            P("store", "seq"),
            P(None, ("seq", "store")),
            P(("seq", "store"), None),
        ),
        out_specs=P("store", "seq", None),
        check_vma=False,
    )
```

```python
import functools

import jax
import jax.numpy as jnp
from jax import lax
from jax.experimental import pallas as pl
from jax.experimental.pallas import tpu as pltpu
from jax.sharding import PartitionSpec as P

HEAD_DIM = 128
HEADS = 32
KV_HEADS = 4
RANK = 64
EXP_DEV = 16
GROUPS = 4
HOPS = 2
SEG_ROWS = 16
MESH = pl.DeviceIdType.MESH


def gather_kernel(n_seq, own_ref, out_ref, local_sem, send_sem, recv_sem):
    per = n_seq // GROUPS
    me = lax.axis_index("seq")
    st = lax.axis_index("store")
    level = me // per
    bits = []
    bit = 2
    while bit < per:
        bits.append(bit)
        bit *= 2
    bits.append(1)

    def flip(b, index=None):
        index = me if index is None else index
        return index + b - 2 * b * ((index // b) % 2)

    barrier = pltpu.get_barrier_semaphore()
    for b in bits:
        pl.semaphore_signal(barrier, inc=1, device_id=(flip(b), st), device_id_type=MESH)

    @pl.when(level < GROUPS - 1)
    def _():
        pl.semaphore_signal(barrier, inc=1, device_id=(me + per, st), device_id_type=MESH)

    @pl.when(level > 0)
    def _():
        pl.semaphore_signal(barrier, inc=1, device_id=(me - per, st), device_id_type=MESH)

    ends = (level < GROUPS - 1).astype(jnp.int32) + (level > 0).astype(jnp.int32)
    pl.semaphore_wait(barrier, len(bits) + ends)

    def remote(source, block, target, sem):
        return pltpu.make_async_remote_copy(
            src_ref=source,
            dst_ref=out_ref.at[block],
            send_sem=send_sem.at[sem],
            recv_sem=recv_sem.at[sem],
            device_id=(target, st),
            device_id_type=MESH,
        )

    def guarded(condition, act):
        if condition is None:
            act()
        else:
            pl.when(condition)(act)

    steps = []
    sem = HOPS
    for hop in range(HOPS + 1):
        masks = [0]
        for b in bits:
            for m in masks:
                steps.append((sem, m, hop, b))
                sem += 1
            masks = masks + [m ^ b for m in masks]

    def column(m):
        index = me
        for b in bits:
            if m & b:
                index = flip(b, index)
        return index

    def at(m, hop):
        return jnp.maximum(column(m) - hop * per, 0)

    def block_ref(m, hop):
        return own_ref if (m == 0 and hop == 0) else out_ref.at[at(m, hop)]

    mine = pltpu.make_async_copy(own_ref, out_ref.at[me], local_sem)
    mine.start()
    up = jnp.minimum(me + per, n_seq - 1)

    def z_copy(hop):
        return remote(block_ref(0, hop), at(0, hop), up, hop)

    def z_arrival(hop):
        return remote(block_ref(0, hop), at(0, hop), up, hop - 1)

    def x_copy(step):
        s, m, hop, b = step
        return remote(block_ref(m, hop), at(m, hop), flip(b), s)

    def x_arrival(step):
        s, m, hop, b = step
        ref = out_ref.at[jnp.maximum(flip(b, column(m)) - hop * per, 0)]
        return pltpu.make_async_remote_copy(
            src_ref=ref, dst_ref=ref, send_sem=send_sem.at[s], recv_sem=recv_sem.at[s],
            device_id=(flip(b), st), device_id_type=MESH,
        )

    z_conditions = [(level < GROUPS - 1) & (level >= hop) for hop in range(HOPS)]
    guarded(z_conditions[0], lambda: z_copy(0).start())
    for hop in range(HOPS + 1):
        condition = None if hop == 0 else level >= hop
        if hop > 0:
            arrived = z_arrival(hop)
            guarded(condition, arrived.wait_recv)
            if hop < HOPS:
                guarded(z_conditions[hop], z_copy(hop).start)
        group = [s for s in steps if s[2] == hop]

        first = [s for s in group if s[1] == 0]

        def begin(first=first):
            for s in first:
                x_copy(s).start()

        guarded(condition, begin)
    for hop in range(HOPS + 1):
        condition = None if hop == 0 else level >= hop
        group = [s for s in steps if s[2] == hop]

        def rest(group=group):
            have = {0}
            waiting = list(group)
            for position, b in enumerate(bits):
                stage = [s for s in waiting if s[3] == b]
                for s in stage:
                    if s[1] != 0:
                        x_copy(s).start()
                for s in stage:
                    x_arrival(s).wait_recv()
            for s in group:
                x_copy(s).wait_send()

        guarded(condition, rest)
    for hop in range(HOPS):
        guarded(z_conditions[hop], z_copy(hop).wait_send)
    mine.wait()


def gather_blocks(block, n_seq):
    per = n_seq // GROUPS
    copies = HOPS + (HOPS + 1) * (per - 1)
    return pl.pallas_call(
        functools.partial(gather_kernel, n_seq),
        out_shape=jax.ShapeDtypeStruct((n_seq,) + block.shape, block.dtype),
        in_specs=[pl.BlockSpec(memory_space=pl.ANY)],
        out_specs=pl.BlockSpec(memory_space=pl.ANY),
        scratch_shapes=[
            pltpu.SemaphoreType.DMA,
            pltpu.SemaphoreType.DMA((copies,)),
            pltpu.SemaphoreType.DMA((copies,)),
        ],
        compiler_params=pltpu.CompilerParams(collective_id=1, has_side_effects=True),
        name="gather_blocks",
    )(block)


def routed_kernel(
    n_store, devices, cap,
    q_ref, kv_ref, qseg_ref, place_ref, tags_ref, down_hbm, up_hbm,
    out_ref,
    weight_ref, ctx_ref, m_ref, l_ref, acc_ref, send_ref, got_ref, ans_ref, tag_ref, total_ref, low_ref,
    load_sem, send_sem, recv_sem,
):
    tok = q_ref.shape[0]
    n_seq = kv_ref.shape[0]
    group = HEADS // KV_HEADS
    part = group * HEAD_DIM
    split = SEG_ROWS // cap
    piece = part // split
    slots = devices * cap
    packed = devices * SEG_ROWS
    me = lax.axis_index("seq")
    flat = me * n_store + lax.axis_index("store")
    coef = (HEAD_DIM**-0.5) * 1.4426950408889634

    up_at = weight_ref.shape[0] - 1

    def load_down(g):
        rows = pl.ds(pl.multiple_of(g * part, part), part)
        return pltpu.make_async_copy(down_hbm.at[rows], weight_ref.at[0, g], load_sem.at[g])

    def load_up(g):
        cols = pl.ds(pl.multiple_of(g * part, part), part)
        return pltpu.make_async_copy(up_hbm.at[:, cols], weight_ref.at[up_at, g], load_sem.at[KV_HEADS + g])

    @pl.loop(0, KV_HEADS)
    def _(g):
        load_down(g).start()
        if up_at:
            load_up(g).start()

    barrier = pltpu.get_barrier_semaphore()

    @pl.loop(1, devices)
    def _(p):
        peer = (flat + p) % devices
        pl.semaphore_signal(barrier, inc=1, device_id=(peer // n_store, peer % n_store), device_id_type=MESH)

    pl.semaphore_wait(barrier, devices - 1)

    def exchange(source, target, sem):
        @pl.loop(1, devices)
        def _(p):
            peer = (flat + p) % devices
            pltpu.make_async_remote_copy(
                src_ref=source.at[peer], dst_ref=target.at[flat], send_sem=send_sem.at[sem], recv_sem=recv_sem.at[sem],
                device_id=(peer // n_store, peer % n_store), device_id_type=MESH,
            ).start()

    def all_of(source, target, sem):
        others = pl.ds(0, devices - 1)
        return pltpu.make_async_remote_copy(
            src_ref=source.at[others], dst_ref=target.at[others], send_sem=send_sem.at[sem], recv_sem=recv_sem.at[sem],
            device_id=((me + 1) % n_seq, lax.axis_index("store")), device_id_type=MESH,
        )

    exchange(tags_ref, tag_ref, 2 * KV_HEADS)
    tag_ref[flat] = tags_ref[flat]

    def segment_column(block):
        row = kv_ref[block, tok : tok + SEG_ROWS, :tok].astype(jnp.float32)[0:1]
        return jnp.broadcast_to(row, (tok, tok)).T

    @pl.loop(0, KV_HEADS)
    def _(g):
        start = pl.multiple_of(g * part, part)
        q_all = q_ref[:, pl.ds(start, part)]
        q = jnp.concatenate([q_all[:, h * HEAD_DIM : (h + 1) * HEAD_DIM] for h in range(group)], axis=0)
        m_ref[...] = jnp.full_like(m_ref, -1e30)
        l_ref[...] = jnp.zeros_like(l_ref)
        acc_ref[...] = jnp.zeros_like(acc_ref)
        k_cols = pl.ds(pl.multiple_of(g * HEAD_DIM, HEAD_DIM), HEAD_DIM)
        v_cols = pl.ds(pl.multiple_of((KV_HEADS + g) * HEAD_DIM, HEAD_DIM), HEAD_DIM)

        @pl.loop(jnp.maximum(me - n_seq // HOPS, 0) // 2, me // 2 + 1)
        def _(pair):
            k = kv_ref[pl.ds(2 * pair, 2), :tok, k_cols].reshape(2 * tok, HEAD_DIM)
            v = kv_ref[pl.ds(2 * pair, 2), :tok, v_cols].reshape(2 * tok, HEAD_DIM)
            s = lax.dot_general(k, q, (((1,), (1,)), ((), ())), preferred_element_type=jnp.float32)
            key_pos = 2 * pair * tok + lax.broadcasted_iota(jnp.int32, (2 * tok, tok), 0)
            q_pos = me * tok + lax.broadcasted_iota(jnp.int32, (2 * tok, tok), 1)
            kseg = jnp.concatenate([segment_column(2 * pair), segment_column(2 * pair + 1)], axis=0)
            seen = (key_pos <= q_pos) & (kseg == qseg_ref[...])
            bias = jnp.where(seen, 0.0, -1e30).astype(jnp.float32)
            s = s + jnp.concatenate([bias] * group, axis=1)
            m_old = m_ref[...]
            m_new = jnp.maximum(m_old, jnp.max(s, axis=0, keepdims=True))
            alpha = jnp.exp2((m_old - m_new) * coef)
            p = jnp.exp2((s - m_new) * coef)
            m_ref[...] = m_new
            l_ref[...] = l_ref[...] * alpha + jnp.sum(p, axis=0, keepdims=True)
            pv = lax.dot_general(
                v, p.astype(jnp.bfloat16), (((0,), (0,)), ((), ())), preferred_element_type=jnp.float32
            )
            acc_ref[...] = acc_ref[...] * alpha + pv

        out = acc_ref[...] / l_ref[...]
        ctx = jnp.concatenate([out[:, h * tok : (h + 1) * tok].T for h in range(group)], axis=1).astype(jnp.bfloat16)
        ctx_ref[:, pl.ds(start, part)] = ctx
        stacked = jnp.concatenate([ctx[:, i * piece : (i + 1) * piece] for i in range(split)], axis=0)
        rows = jnp.dot(place_ref[...], stacked, preferred_element_type=jnp.float32).astype(jnp.bfloat16)
        send_ref[g] = rows.reshape(devices, SEG_ROWS, piece)
        exchange(send_ref.at[g], got_ref.at[g], g)
        got_ref[g, flat] = send_ref[g, flat]

    def chosen_rows(i):
        row = lax.broadcasted_iota(jnp.int32, (slots, 1), 0)
        column = lax.broadcasted_iota(jnp.int32, (1, packed), 1)
        wanted = (row // cap) * SEG_ROWS + i * cap + row % cap
        return jnp.where(column == wanted, 1.0, 0.0).astype(jnp.bfloat16)

    total_ref[...] = jnp.zeros_like(total_ref)
    all_of(tags_ref, tag_ref, 2 * KV_HEADS).wait()

    @pl.loop(0, KV_HEADS)
    def _(g):
        all_of(send_ref.at[g], got_ref.at[g], g).wait_recv()
        load_down(g).wait()
        got = got_ref[g].reshape(packed, piece)
        for i in range(split):
            rows = jnp.dot(chosen_rows(i), got, preferred_element_type=jnp.float32).astype(jnp.bfloat16)
            total_ref[...] += jnp.dot(rows, weight_ref[0, g, pl.ds(i * piece, piece)], preferred_element_type=jnp.float32)

    tags = jnp.dot(chosen_rows(0), tag_ref[...].reshape(packed, HEAD_DIM), preferred_element_type=jnp.float32)
    held = total_ref.shape[1]
    lane = lax.broadcasted_iota(jnp.int32, (slots, held), 1) // RANK + 1
    tags = jnp.concatenate([tags] * (held // HEAD_DIM), axis=1)
    low_ref[...] = jnp.where(tags == lane.astype(jnp.float32), total_ref[...], 0.0).astype(jnp.bfloat16)
    if not up_at:

        @pl.loop(0, KV_HEADS)
        def _(g):
            load_up(g).start()

    @pl.loop(0, KV_HEADS)
    def _(g):
        load_up(g).wait()
        delta = jnp.dot(low_ref[...], weight_ref[up_at, g], preferred_element_type=jnp.float32).astype(jnp.bfloat16)
        rows = jnp.zeros((packed, piece), jnp.float32)
        for i in range(split):
            rows += lax.dot_general(
                chosen_rows(i), delta[:, i * piece : (i + 1) * piece], (((0,), (0,)), ((), ())),
                preferred_element_type=jnp.float32,
            )
        all_of(send_ref.at[g], got_ref.at[g], g).wait_send()
        send_ref[g] = rows.astype(jnp.bfloat16).reshape(devices, SEG_ROWS, piece)
        exchange(send_ref.at[g], ans_ref.at[g], KV_HEADS + g)
        ans_ref[g, flat] = send_ref[g, flat]

    @pl.loop(0, KV_HEADS)
    def _(g):
        all_of(send_ref.at[g], ans_ref.at[g], KV_HEADS + g).wait_recv()
        rows = ans_ref[g].reshape(packed, piece)
        delta = jnp.concatenate(
            [
                lax.dot_general(
                    place_ref[:, i * tok : (i + 1) * tok], rows, (((0,), (0,)), ((), ())),
                    preferred_element_type=jnp.float32,
                )
                for i in range(split)
            ],
            axis=1,
        )
        cols = pl.ds(pl.multiple_of(g * part, part), part)
        out_ref[:, cols] = (ctx_ref[:, cols].astype(jnp.float32) + delta).astype(jnp.bfloat16)

    @pl.loop(0, KV_HEADS)
    def _(g):
        all_of(send_ref.at[g], ans_ref.at[g], KV_HEADS + g).wait_send()


def routed(n_store, devices, cap, queries, blocks, qseg, place, tags, down, up):
    tok, width = queries.shape
    part = width // KV_HEADS
    held = down.shape[1]
    cols = tok * (HEADS // KV_HEADS)
    wire = (KV_HEADS, devices, SEG_ROWS, part * cap // SEG_ROWS)
    vmem = pl.BlockSpec(memory_space=pltpu.VMEM)
    hbm = pl.BlockSpec(memory_space=pl.ANY)
    return pl.pallas_call(
        functools.partial(routed_kernel, n_store, devices, cap),
        out_shape=jax.ShapeDtypeStruct((tok, width), jnp.bfloat16),
        in_specs=[vmem] * 5 + [hbm] * 2,
        out_specs=vmem,
        scratch_shapes=[
            pltpu.VMEM((2 if devices <= 32 else 1, KV_HEADS, part, held), jnp.bfloat16),
            pltpu.VMEM((tok, width), jnp.bfloat16),
            pltpu.VMEM((1, cols), jnp.float32),
            pltpu.VMEM((1, cols), jnp.float32),
            pltpu.VMEM((HEAD_DIM, cols), jnp.float32),
            pltpu.VMEM(wire, jnp.bfloat16),
            pltpu.VMEM(wire, jnp.bfloat16),
            pltpu.VMEM(wire, jnp.bfloat16),
            pltpu.VMEM(tags.shape, jnp.bfloat16),
            pltpu.VMEM((devices * cap, held), jnp.float32),
            pltpu.VMEM((devices * cap, held), jnp.bfloat16),
            pltpu.SemaphoreType.DMA((2 * KV_HEADS,)),
            pltpu.SemaphoreType.DMA((2 * KV_HEADS + 1,)),
            pltpu.SemaphoreType.DMA((2 * KV_HEADS + 1,)),
        ],
        compiler_params=pltpu.CompilerParams(collective_id=2, has_side_effects=True, vmem_limit_bytes=62 << 20),
        name="routed",
    )(queries, blocks, qseg, place, tags, down, up)


def local(queries, keys, values, segment_ids, route_ids, adapter_down, adapter_up):
    n_seq = lax.axis_size("seq")
    n_store = lax.axis_size("store")
    tok = queries.shape[1]
    seg = segment_ids[0].astype(jnp.bfloat16)
    seg_row = jnp.pad(seg[None, :], ((0, SEG_ROWS - 1), (0, keys.shape[2] * 2 - tok)))
    own = jnp.concatenate([jnp.concatenate([keys[0], values[0]], axis=1), seg_row], axis=0)
    blocks = gather_blocks(own, n_seq)

    devices = n_seq * n_store
    capacity = max(2, 2 * tok // devices)
    split = SEG_ROWS // capacity
    chosen = route_ids[0]
    owners = chosen // EXP_DEV
    one_hot = (owners[:, None] == jnp.arange(devices, dtype=jnp.int32)[None, :]).astype(jnp.bfloat16)
    lower = jnp.tril(jnp.ones((tok, tok), jnp.bfloat16))
    counts = jnp.dot(lower, one_hot, preferred_element_type=jnp.float32)
    slot_of = jnp.sum(counts * one_hot.astype(jnp.float32), axis=1).astype(jnp.int32) - 1
    placed = owners * SEG_ROWS + slot_of
    packed = jnp.arange(devices * SEG_ROWS, dtype=jnp.int32)[:, None]
    place = (packed == jnp.concatenate([placed + i * capacity for i in range(split)])[None, :]).astype(jnp.bfloat16)
    names = (chosen % EXP_DEV + 1).astype(jnp.bfloat16)
    tags = jnp.dot(
        place[:, :tok], jnp.broadcast_to(names[:, None], (tok, HEAD_DIM)), preferred_element_type=jnp.float32
    ).astype(jnp.bfloat16)
    tags = tags.reshape(devices, SEG_ROWS, HEAD_DIM)

    qseg = seg.astype(jnp.float32)[None, :]
    return routed(
        n_store, devices, capacity, queries[0], blocks, qseg, place, tags, adapter_down, adapter_up
    )[None]


def solution(mesh):
    return jax.shard_map(
        local,
        mesh=mesh,
        in_specs=(
            P("store", "seq", None),
            P("store", "seq", None),
            P("store", "seq", None),
            P("store", "seq"),
            P("store", "seq"),
            P(None, ("seq", "store")),
            P(("seq", "store"), None),
        ),
        out_specs=P("store", "seq", None),
        check_vma=False,
    )
```
